32 devices in a mesh: genome: 8 (over z, x), samp: 4 (over y, core).
Axes of the slice: x: 2, y: 2, z: 4, core: 2. Of those that a mesh axis runs over, the one named last changes fastest.
Arguments:
- dosage: bfloat16 [16384, 8192], P('samp', 'genome'), may hold values from -6 to 6
- effects: bfloat16 [8192, 512], P('genome', 'samp'), may hold values from -6 to 6
- depth: int32 [32], P('genome'), may hold values from 1 to 4
Outputs:
- ld_effects: float32 [8192, 512], P('genome', 'samp')
The draws below stay inside these ranges and needn't reach their ends.
Inputs may be any that keep to these rules, and one draw needn't show every extreme that they name: Every block's window depth lies between 1 and 4.
All inputs are finite; a program needn't handle non-finite values.
Results may differ from the reference program's by a relative error of at most 0.0029.
Values may be sent and summed in bfloat16 or wider, within the bound.
A program may use at most 128 MiB of HBM per device.

```python
import jax
import jax.numpy as jnp
from jax import lax

BLK = 256
MAXDEPTH = 4
TRAITS = 512
SAMPLES = 16384
NBLOCKS = 32
VARIANTS = 8192


def plant(entries, own_key, least, largest):
    longest = entries.shape.index(max(entries.shape))
    spots = []
    for shift in (0, 1):
        where = [jax.random.randint(jax.random.fold_in(own_key, axis), (), 0, length) for axis, length in enumerate(entries.shape)]
        where[longest] = (where[longest] + shift) % entries.shape[longest]
        spots.append(tuple(where))
    return entries.at[spots[0]].set(least).at[spots[1]].set(largest)


def block_scale(own_key, extent, shards, smallest, largest):
    loudness = 1.0
    for position, blocks in shards:
        draws = jax.random.uniform(jax.random.fold_in(jax.random.fold_in(own_key, 6), position), (blocks,), jnp.float32, smallest / len(shards), largest / len(shards))
        loudness = loudness * jnp.repeat(jnp.exp(draws), extent[position] // blocks).reshape((-1,) + (1,) * (len(extent) - 1 - position))
    return loudness


def scatter_about(stream_key, shape, spread, bound, split=(), kind=jnp.bfloat16):
    entries = spread * jax.random.normal(stream_key, shape, jnp.float32)
    if split:
        entries = entries * block_scale(stream_key, shape, split, -0.22, 0.18)
    return jnp.clip(entries, -bound, bound).astype(kind)


def setup_inputs(seed: int = 0) -> dict:
    arg_keys = jax.random.split(jax.random.key(seed), 4)
    return {
        "dosage": scatter_about(arg_keys[0], (SAMPLES, VARIANTS), 1.0, 6.0, ((0, 4), (1, 8))),
        "effects": scatter_about(arg_keys[1], (VARIANTS, TRAITS), 1.0, 6.0, ((0, 8), (1, 4))),
        "depth": plant(jax.random.randint(arg_keys[2], (NBLOCKS,), 1, 5), jax.random.fold_in(arg_keys[2], 1), 1, 4).astype(jnp.int32),
    }


def reference(dosage, effects, depth):
    span = MAXDEPTH + 1
    padded_x = jnp.pad(dosage, ((0, 0), (0, MAXDEPTH * BLK)))
    padded_b = jnp.pad(effects, ((0, MAXDEPTH * BLK), (0, 0)))
    column_block = jnp.arange(span * BLK, dtype=jnp.int32) // BLK

    def one_block(index):
        start = (index * BLK).astype(jnp.int32)
        own_x = lax.dynamic_slice_in_dim(dosage, start, BLK, 1)
        window_x = lax.dynamic_slice_in_dim(padded_x, start, span * BLK, 1)
        gram = lax.dot_general(own_x, window_x, (((0,), (0,)), ((), ())), preferred_element_type=jnp.float32)
        gram = gram / jnp.float32(SAMPLES)
        keep = (column_block <= depth[index]).astype(jnp.float32)
        corr = (gram * keep[None, :]).astype(jnp.bfloat16)
        window_b = lax.dynamic_slice_in_dim(padded_b, start, span * BLK, 0)
        forward = jnp.dot(corr, window_b, preferred_element_type=jnp.float32)
        own_b = lax.dynamic_slice_in_dim(effects, start, BLK, 0)
        backward = lax.dot_general(corr[:, BLK:], own_b, (((0,), (0,)), ((), ())), preferred_element_type=jnp.float32)
        return forward, backward.reshape(MAXDEPTH, BLK, TRAITS)

    forward, backward = lax.map(one_block, jnp.arange(NBLOCKS, dtype=jnp.int32))
    total = forward
    for offset in range(1, span):
        moved = jnp.pad(backward[:, offset - 1], ((offset, 0), (0, 0), (0, 0)))[:NBLOCKS]
        total = total + moved
    return total.reshape(VARIANTS, TRAITS)
```

```python
import functools

import jax
import jax.numpy as jnp
from jax import lax
from jax.experimental import pallas as pl
from jax.experimental.pallas import tpu as pltpu
from jax.sharding import PartitionSpec as P

BLK = 256
MESH = pl.DeviceIdType.MESH
F32 = jnp.float32
BF16 = jnp.bfloat16
CONTRACT0 = (((0,), (0,)), ((), ()))


def gram(left, right):
    return lax.dot_general(left, right, CONTRACT0, preferred_element_type=F32)


def kernel(
    n_genome, n_samp, nb, half, traits, scale,
    x_ref, e_ref, d_ref, out_ref,
    own, xbuf, zbuf, eff, dep, loc, cro, par, far, stage, rs_loc, rs, hop_out, hop_in,
    own_sem, own_e_sem, x_send, x_recv, z_send, z_recv, es_send, es_recv, ex_send, ex_recv,
    ds_send, ds_recv, ef_send, ef_recv, rl_send, rl_recv, rs_send, rs_recv, h_send, h_recv,
):
    g = lax.axis_index("genome")
    s = lax.axis_index("samp")
    q = lax.rem(g, 2)
    sign = 1 - 2 * q
    partner = g + sign
    z_from = g + 2 * sign
    z_to = g - 2 * sign
    has_from = jnp.logical_and(z_from >= 0, z_from < n_genome)
    has_to = jnp.logical_and(z_to >= 0, z_to < n_genome)

    def mine(u):
        return u + q * (nb - 1 - 2 * u)

    def other(u):
        return nb - 1 - mine(u)

    def peer(d):
        return lax.rem(s + d, n_samp)

    def cols(t):
        return pl.ds(pl.multiple_of(t * traits, traits), traits)

    my_cols = cols(s)
    keep_rows = pl.ds(pl.multiple_of(q * half, half), half)
    give_rows = pl.ds(pl.multiple_of((1 - q) * half, half), half)

    def remote(src, dst, ss, rsem, gg, sss):
        return pltpu.make_async_remote_copy(
            src_ref=src, dst_ref=dst, send_sem=ss, recv_sem=rsem,
            device_id=(gg, sss), device_id_type=MESH,
        )

    barrier = pltpu.get_barrier_semaphore()
    for d in range(1, n_samp):
        pl.semaphore_signal(barrier, inc=1, device_id=(g, peer(d)), device_id_type=MESH)
    pl.semaphore_signal(barrier, inc=1, device_id=(partner, s), device_id_type=MESH)

    @pl.when(has_from)
    def _():
        pl.semaphore_signal(barrier, inc=1, device_id=(z_from, s), device_id_type=MESH)

    @pl.when(has_to)
    def _():
        pl.semaphore_signal(barrier, inc=1, device_id=(z_to, s), device_id_type=MESH)

    own_copies = [
        pltpu.make_async_copy(x_ref.at[:, b * BLK : (b + 1) * BLK], own.at[b], own_sem.at[b])
        for b in range(nb)
    ]
    own_e = pltpu.make_async_copy(e_ref, eff.at[0, :, my_cols], own_e_sem.at[0])
    own_e.start()
    for c in own_copies:
        c.start()
    pl.semaphore_wait(
        barrier, n_samp + has_from.astype(jnp.int32) + has_to.astype(jnp.int32)
    )

    def block_cols(b):
        return pl.ds(pl.multiple_of(b * BLK, BLK), BLK)

    x_copies = [
        remote(x_ref.at[give_rows, block_cols(other(t))], xbuf.at[t], x_send.at[t], x_recv.at[t], partner, s)
        for t in range(nb)
    ]
    z_copies = [
        remote(x_ref.at[keep_rows, block_cols(mine(t))], zbuf.at[t], z_send.at[t], z_recv.at[t], z_to, s)
        for t in range(nb)
    ]
    d_x = remote(d_ref, dep.at[0], ds_send.at[0], ds_recv.at[0], partner, s)
    d_z = remote(d_ref, dep.at[1], ds_send.at[1], ds_recv.at[1], z_to, s)
    e_x = remote(e_ref, eff.at[1, :, my_cols], ex_send.at[0], ex_recv.at[0], partner, s)
    e_z = remote(e_ref, eff.at[2, :, my_cols], ex_send.at[1], ex_recv.at[1], z_to, s)
    d_x.start()
    e_x.start()
    x_copies[0].start()
    x_copies[1].start()

    @pl.when(has_to)
    def _():
        d_z.start()
        e_z.start()
        z_copies[0].start()
        z_copies[1].start()

    e_s = [
        remote(e_ref, eff.at[0, :, my_cols], es_send.at[d - 1], es_recv.at[d - 1], g, peer(d))
        for d in range(1, n_samp)
    ]
    for c in e_s:
        c.start()

    loc[...] = jnp.zeros_like(loc)
    cro[...] = jnp.zeros_like(cro)
    par[...] = jnp.zeros_like(par)
    far[...] = jnp.zeros_like(far)
    own_e.wait()
    for c in own_copies:
        c.wait()
    for c in e_s:
        c.wait()
    e_x.wait_recv()
    f_x = [
        remote(eff.at[1, :, my_cols], eff.at[1, :, my_cols], ef_send.at[d - 1], ef_recv.at[d - 1], g, peer(d))
        for d in range(1, n_samp)
    ]
    for c in f_x:
        c.start()
    f_z = [
        remote(
            eff.at[2, :, my_cols], eff.at[2, :, my_cols],
            ef_send.at[n_samp + d - 2], ef_recv.at[n_samp + d - 2], g, peer(d),
        )
        for d in range(1, n_samp)
    ]

    @pl.when(has_from)
    def _():
        e_z.wait_recv()
        for c in f_z:
            c.start()

    def rows(b):
        return pl.ds(pl.multiple_of(b * BLK, BLK), BLK)

    def weight(drow, k):
        return jnp.where(drow >= k.astype(F32), F32(scale), F32(0.0))

    def local_row(i, carry):
        def local_pair(j, carry):
            full = gram(own[i, :half], own[j, :half]) + gram(own[i, half:], own[j, half:])
            full = full * weight(d_ref[pl.ds(i, 1), :], j - i)
            high = full.astype(BF16)
            low = (full - high.astype(F32)).astype(BF16)
            ej = eff[0, rows(j), :]
            loc[rows(i), :] += jnp.dot(high, ej, preferred_element_type=F32) + jnp.dot(
                low, ej, preferred_element_type=F32
            )

            @pl.when(j > i)
            def _():
                ei = eff[0, rows(i), :]
                loc[rows(j), :] += gram(high, ei) + gram(low, ei)

            return carry

        return lax.fori_loop(i, nb, local_pair, carry)

    lax.fori_loop(0, nb, local_row, 0)
    rl = [
        remote(loc.at[:, cols(peer(d))], rs_loc.at[d - 1], rl_send.at[d - 1], rl_recv.at[d - 1], g, peer(d))
        for d in range(1, n_samp)
    ]
    for c in rl:
        c.start()

    for c in f_x:
        c.wait_recv()
    d_x.wait_recv()

    @pl.when(has_from)
    def _():
        for c in f_z:
            c.wait_recv()
        d_z.wait_recv()

    kinds = {"own": (0, cro), "partner": (1, par), "far": (2, far)}

    def scatter(kind, t):
        n, _ = kinds[kind]
        return [
            remote(
                stage.at[n, t, :, cols(peer(d))], rs.at[n, t, d - 1],
                rs_send.at[n, t, d - 1], rs_recv.at[n, t, d - 1], g, peer(d),
            )
            for d in range(1, n_samp)
        ]

    def publish(kind, t):
        n, acc = kinds[kind]
        stage[n, t] = acc[t * BLK : (t + 1) * BLK, :].astype(BF16)
        for c in scatter(kind, t):
            c.start()

    def collect(kind, t):
        n, acc = kinds[kind]
        for c in scatter(kind, t):
            c.wait_recv()
        total = acc[t * BLK : (t + 1) * BLK, my_cols]
        for d in range(1, n_samp):
            total = total + rs[n, t, d - 1].astype(F32)
        return total

    def hop(n, t):
        return remote(
            hop_out.at[n, t], hop_in.at[n, t], h_send.at[n, t], h_recv.at[n, t],
            partner if n == 0 else z_from, s,
        )

    def forward(n, t):
        hop_out[n, t] = collect("partner" if n == 0 else "far", t).astype(BF16)
        hop(n, t).start()

    for t in range(nb):
        x_copies[t].wait_recv()
        if t + 2 < nb:
            x_copies[t].wait_send()
            x_copies[t + 2].start()

            @pl.when(has_to)
            def _():
                z_copies[t].wait_send()
                z_copies[t + 2].start()

        def x_pair(u, carry):
            k = nb + t - u
            mu, mt = mine(u), mine(t)
            drow = jnp.where(q == 0, d_ref[pl.ds(mu, 1), :], dep[0, pl.ds(mt, 1), :])
            full = gram(own[mu, keep_rows, :], xbuf[t]) * weight(drow, k)
            high = full.astype(BF16)
            cro[rows(u), :] += jnp.dot(high, eff[1, rows(other(nb - 1 - t)), :], preferred_element_type=F32)
            par[t * BLK : (t + 1) * BLK, :] += gram(high, eff[0, rows(mu), :])
            return carry

        lax.fori_loop(t, nb, x_pair, 0)
        publish("own", t)

        @pl.when(has_from)
        def _():
            z_copies[t].wait_recv()

            def z_pair(v, carry):
                k = nb + v - t
                mt, mv = mine(t), mine(v)
                drow = jnp.where(q == 0, dep[0, pl.ds(mt, 1), :], dep[1, pl.ds(mv, 1), :])
                full = gram(xbuf[t], zbuf[v]) * weight(drow, jnp.int32(0) + k)
                high = full.astype(BF16)
                par[t * BLK : (t + 1) * BLK, :] += jnp.dot(high, eff[2, rows(mv), :], preferred_element_type=F32)
                far[rows(v), :] += gram(high, eff[1, rows(mt), :])
                return carry

            lax.fori_loop(0, t + 1, z_pair, 0)

        publish("partner", t)
        if t > 0:
            forward(0, t - 1)

    @pl.when(has_from)
    def _():
        for v in range(nb):
            publish("far", v)
    forward(0, nb - 1)

    for c in rl:
        c.wait_recv()
    total = loc[:, my_cols]
    for d in range(1, n_samp):
        total = total + rs_loc[d - 1]
    out_ref[...] = total
    for t in range(nb):
        part = collect("own", t)
        out_ref[rows(mine(t)), :] += part

    @pl.when(has_from)
    def _():
        for v in range(nb):
            forward(1, v)
    for t in range(nb):
        hop(0, t).wait_recv()
        out_ref[rows(other(t)), :] += hop_in[0, t].astype(F32)

    @pl.when(has_to)
    def _():
        for v in range(nb):
            hop(1, v).wait_recv()
            out_ref[rows(mine(v)), :] += hop_in[1, v].astype(F32)

    d_x.wait_send()
    e_x.wait_send()
    for t in range(nb - 2, nb):
        x_copies[t].wait_send()

    @pl.when(has_to)
    def _():
        d_z.wait_send()
        e_z.wait_send()
        for t in range(nb - 2, nb):
            z_copies[t].wait_send()

    for c in f_x + rl:
        c.wait_send()
    for t in range(nb):
        for c in scatter("own", t) + scatter("partner", t):
            c.wait_send()
        hop(0, t).wait_send()

    @pl.when(has_from)
    def _():
        for c in f_z:
            c.wait_send()
        for t in range(nb):
            for c in scatter("far", t):
                c.wait_send()
            hop(1, t).wait_send()


def body(n_genome, n_samp, dosage, effects, depth):
    nb = depth.shape[0]
    samples, variants = dosage.shape
    traits = effects.shape[1]
    all_traits = traits * n_samp
    half = samples // 2
    d = jnp.zeros((8, BLK), F32).at[:nb].set(jnp.broadcast_to(depth.astype(F32)[:, None], (nb, BLK)))
    dma = pltpu.SemaphoreType.DMA
    p = n_samp - 1
    return pl.pallas_call(
        functools.partial(kernel, n_genome, n_samp, nb, half, traits, 1.0 / (samples * n_samp)),
        out_shape=jax.ShapeDtypeStruct((variants, traits), F32),
        in_specs=[
            pl.BlockSpec(memory_space=pl.ANY),
            pl.BlockSpec(memory_space=pl.ANY),
            pl.BlockSpec(memory_space=pltpu.VMEM),
        ],
        out_specs=pl.BlockSpec(memory_space=pltpu.VMEM),
        scratch_shapes=[
            pltpu.VMEM((nb, samples, BLK), BF16),
            pltpu.VMEM((nb, half, BLK), BF16),
            pltpu.VMEM((nb, half, BLK), BF16),
            pltpu.VMEM((3, variants, all_traits), BF16),
            pltpu.VMEM((2, 8, BLK), F32),
            pltpu.VMEM((variants, all_traits), F32),
            pltpu.VMEM((variants, all_traits), F32),
            pltpu.VMEM((variants, all_traits), F32),
            pltpu.VMEM((variants, all_traits), F32),
            pltpu.VMEM((3, nb, BLK, all_traits), BF16),
            pltpu.VMEM((p, variants, traits), F32),
            pltpu.VMEM((3, nb, p, BLK, traits), BF16),
            pltpu.VMEM((2, nb, BLK, traits), BF16),
            pltpu.VMEM((2, nb, BLK, traits), BF16),
            dma((nb,)), dma((1,)),
            dma((nb,)), dma((nb,)), dma((nb,)), dma((nb,)),
            dma((p,)), dma((p,)),
            dma((2,)), dma((2,)), dma((2,)), dma((2,)),
            dma((2 * p,)), dma((2 * p,)),
            dma((p,)), dma((p,)),
            dma((3, nb, p)), dma((3, nb, p)),
            dma((2, nb)), dma((2, nb)),
        ],
        compiler_params=pltpu.CompilerParams(
            collective_id=0, has_side_effects=True, vmem_limit_bytes=60 * 1024 * 1024
        ),
        cost_estimate=pl.CostEstimate(
            flops=2 * 20 * BLK * BLK * samples, bytes_accessed=4 * samples * variants, transcendentals=0
        ),
    )(dosage, effects, d)


def solution(mesh):
    return jax.shard_map(
        functools.partial(body, mesh.shape["genome"], mesh.shape["samp"]),
        mesh=mesh,
        in_specs=(P("samp", "genome"), P("genome", "samp"), P("genome")),
        out_specs=P("genome", "samp"),
        check_vma=False,
    )
```

```python
import functools

import jax
import jax.numpy as jnp
from jax import lax
from jax.experimental import pallas as pl
from jax.experimental.pallas import tpu as pltpu
from jax.sharding import PartitionSpec as P

BLK = 256
MESH = pl.DeviceIdType.MESH
F32 = jnp.float32
BF16 = jnp.bfloat16
CONTRACT0 = (((0,), (0,)), ((), ()))


def gram(left, right):
    return lax.dot_general(left, right, CONTRACT0, preferred_element_type=F32)


def kernel(
    n_genome, n_samp, nb, half, traits, scale,
    x_ref, e_ref, d_ref, out_ref,
    own, xbuf, zbuf, eff, dep, loc, cro, par, far, lc_in, ly_out, ly_in, c_in, y_out, y_in, hop_out, hop_in,
    own_sem, own_e_sem, x_send, x_recv, z_send, z_recv, es_send, es_recv, ex_send, ex_recv,
    ds_send, ds_recv, lc_send, lc_recv, ly_send, ly_recv, c_send, c_recv, y_send, y_recv, h_send, h_recv,
):
    g = lax.axis_index("genome")
    s = lax.axis_index("samp")
    q = lax.rem(g, 2)
    sign = 1 - 2 * q
    partner = g + sign
    z_from = g + 2 * sign
    z_to = g - 2 * sign
    has_from = jnp.logical_and(z_from >= 0, z_from < n_genome)
    has_to = jnp.logical_and(z_to >= 0, z_to < n_genome)

    def mine(u):
        return u + q * (nb - 1 - 2 * u)

    def other(u):
        return nb - 1 - mine(u)

    core = lax.rem(s, 2)
    core_mate = s + 1 - 2 * core
    cross_mate = lax.rem(s + 2, n_samp)

    def cols(t):
        return pl.ds(pl.multiple_of(t * traits, traits), traits)

    my_cols = cols(s)
    keep_rows = pl.ds(pl.multiple_of(q * half, half), half)
    give_rows = pl.ds(pl.multiple_of((1 - q) * half, half), half)

    def remote(src, dst, ss, rsem, gg, sss):
        return pltpu.make_async_remote_copy(
            src_ref=src, dst_ref=dst, send_sem=ss, recv_sem=rsem,
            device_id=(gg, sss), device_id_type=MESH,
        )

    barrier = pltpu.get_barrier_semaphore()
    for mate in (core_mate, cross_mate):
        pl.semaphore_signal(barrier, inc=1, device_id=(g, mate), device_id_type=MESH)
    pl.semaphore_signal(barrier, inc=1, device_id=(partner, s), device_id_type=MESH)

    @pl.when(has_from)
    def _():
        pl.semaphore_signal(barrier, inc=1, device_id=(z_from, s), device_id_type=MESH)

    @pl.when(has_to)
    def _():
        pl.semaphore_signal(barrier, inc=1, device_id=(z_to, s), device_id_type=MESH)

    own_copies = [
        pltpu.make_async_copy(x_ref.at[:, b * BLK : (b + 1) * BLK], own.at[b], own_sem.at[b])
        for b in range(nb)
    ]
    own_e = pltpu.make_async_copy(e_ref, eff.at[0, :, my_cols], own_e_sem.at[0])
    own_e.start()
    for c in own_copies:
        c.start()
    pl.semaphore_wait(
        barrier, 3 + has_from.astype(jnp.int32) + has_to.astype(jnp.int32)
    )

    def block_cols(b):
        return pl.ds(pl.multiple_of(b * BLK, BLK), BLK)

    x_copies = [
        remote(x_ref.at[give_rows, block_cols(other(t))], xbuf.at[t], x_send.at[t], x_recv.at[t], partner, s)
        for t in range(nb)
    ]
    z_copies = [
        remote(x_ref.at[keep_rows, block_cols(mine(t))], zbuf.at[t], z_send.at[t], z_recv.at[t], z_to, s)
        for t in range(nb)
    ]
    d_x = remote(d_ref, dep.at[0], ds_send.at[0], ds_recv.at[0], partner, s)
    d_z = remote(d_ref, dep.at[1], ds_send.at[1], ds_recv.at[1], z_to, s)
    e_x = remote(e_ref, eff.at[1, :, my_cols], ex_send.at[0], ex_recv.at[0], partner, s)
    e_z = remote(e_ref, eff.at[2, :, my_cols], ex_send.at[1], ex_recv.at[1], z_to, s)
    d_x.start()
    e_x.start()
    x_copies[0].start()
    x_copies[1].start()

    @pl.when(has_to)
    def _():
        d_z.start()
        e_z.start()
        z_copies[0].start()
        z_copies[1].start()

    def gather(slot, source):
        across = cols(cross_mate)
        here = eff.at[slot, :, my_cols]
        there = eff.at[slot, :, across]
        return [
            remote(source, here, es_send.at[slot, 0], es_recv.at[slot, 0], g, core_mate),
            remote(source, here, es_send.at[slot, 1], es_recv.at[slot, 1], g, cross_mate),
            remote(there, there, es_send.at[slot, 2], es_recv.at[slot, 2], g, core_mate),
        ]

    e_own = gather(0, e_ref)
    e_partner = gather(1, eff.at[1, :, my_cols])
    e_far = gather(2, eff.at[2, :, my_cols])
    e_own[0].start()
    e_own[1].start()
    loc[...] = jnp.zeros_like(loc)
    cro[...] = jnp.zeros_like(cro)
    par[...] = jnp.zeros_like(par)
    far[...] = jnp.zeros_like(far)
    e_own[1].wait_recv()
    e_own[2].start()
    e_x.wait_recv()
    e_partner[0].start()
    e_partner[1].start()

    @pl.when(has_from)
    def _():
        e_z.wait_recv()
        e_far[0].start()
        e_far[1].start()

    own_e.wait()
    for c in own_copies:
        c.wait()
    e_own[0].wait_recv()
    e_own[2].wait_recv()

    def weight(drow, k):
        return jnp.where(drow >= k.astype(F32), F32(scale), F32(0.0))

    def rows(b):
        return pl.ds(pl.multiple_of(b * BLK, BLK), BLK)

    def local_row(i, carry):
        def local_pair(j, carry):
            full = gram(own[i, :half], own[j, :half]) + gram(own[i, half:], own[j, half:])
            full = full * weight(d_ref[pl.ds(i, 1), :], j - i)
            high = full.astype(BF16)
            low = (full - high.astype(F32)).astype(BF16)
            ej = eff[0, rows(j), :]
            loc[rows(i), :] += jnp.dot(high, ej, preferred_element_type=F32) + jnp.dot(
                low, ej, preferred_element_type=F32
            )

            @pl.when(j > i)
            def _():
                ei = eff[0, rows(i), :]
                loc[rows(j), :] += gram(high, ei) + gram(low, ei)

            return carry

        return lax.fori_loop(i, nb, local_pair, carry)

    lax.fori_loop(0, nb, local_row, 0)
    def loc_core(y):
        return remote(
            loc.at[:, cols(2 * y + 1 - core)], lc_in.at[y], lc_send.at[y], lc_recv.at[y], g, core_mate
        )

    loc_across = remote(ly_out, ly_in, ly_send.at[0], ly_recv.at[0], g, cross_mate)
    loc_core(0).start()
    loc_core(1).start()
    e_partner[1].wait_recv()
    e_partner[2].start()
    d_x.wait_recv()

    @pl.when(has_from)
    def _():
        e_far[1].wait_recv()
        e_far[2].start()
        d_z.wait_recv()

    my_y = s // 2
    mate_y = 1 - my_y
    loc_core(0).wait_recv()
    loc_core(1).wait_recv()
    ly_out[...] = loc[:, cols(cross_mate)] + lc_in[mate_y]
    loc_across.start()
    e_partner[0].wait_recv()
    e_partner[2].wait_recv()

    @pl.when(has_from)
    def _():
        e_far[0].wait_recv()
        e_far[2].wait_recv()

    kinds = {"own": (0, cro), "partner": (1, par), "far": (2, far)}

    def block_rows(t):
        return pl.ds(t * BLK, BLK)

    def to_core(kind, t):
        n, acc = kinds[kind]
        return [
            remote(
                acc.at[block_rows(t), cols(2 * y + 1 - core)], c_in.at[n, t, y],
                c_send.at[n, t, y], c_recv.at[n, t, y], g, core_mate,
            )
            for y in range(2)
        ]

    def across(kind, t):
        n, _ = kinds[kind]
        return remote(y_out.at[n, t], y_in.at[n, t], y_send.at[n, t], y_recv.at[n, t], g, cross_mate)

    def publish(kind, t):
        for c in to_core(kind, t):
            c.start()

    def relay(kind, t):
        n, acc = kinds[kind]
        for c in to_core(kind, t):
            c.wait_recv()
        y_out[n, t] = (acc[block_rows(t), cols(cross_mate)] + c_in[n, t, mate_y]).astype(BF16)
        across(kind, t).start()

    def collect(kind, t):
        n, acc = kinds[kind]
        across(kind, t).wait_recv()
        return acc[block_rows(t), my_cols] + c_in[n, t, my_y] + y_in[n, t].astype(F32)

    def hop(n, t):
        return remote(
            hop_out.at[n, t], hop_in.at[n, t], h_send.at[n, t], h_recv.at[n, t],
            partner if n == 0 else z_from, s,
        )

    def forward(n, t):
        hop_out[n, t] = collect("partner" if n == 0 else "far", t).astype(BF16)
        hop(n, t).start()

    for t in range(nb):
        x_copies[t].wait_recv()
        if t + 2 < nb:
            x_copies[t].wait_send()
            x_copies[t + 2].start()

            @pl.when(has_to)
            def _():
                z_copies[t].wait_send()
                z_copies[t + 2].start()

        def x_pair(u, carry):
            k = nb + t - u
            mu, mt = mine(u), mine(t)
            drow = jnp.where(q == 0, d_ref[pl.ds(mu, 1), :], dep[0, pl.ds(mt, 1), :])
            full = gram(own[mu, keep_rows, :], xbuf[t]) * weight(drow, k)
            high = full.astype(BF16)
            cro[rows(u), :] += jnp.dot(high, eff[1, rows(other(nb - 1 - t)), :], preferred_element_type=F32)
            par[t * BLK : (t + 1) * BLK, :] += gram(high, eff[0, rows(mu), :])
            return carry

        if t > 0:
            relay("partner", t - 1)
            relay("own", t - 1)

        @pl.when(has_from)
        def _():
            z_copies[t].wait_recv()

            def z_pair(v, carry):
                k = nb + v - t
                mt, mv = mine(t), mine(v)
                drow = jnp.where(q == 0, dep[0, pl.ds(mt, 1), :], dep[1, pl.ds(mv, 1), :])
                full = gram(xbuf[t], zbuf[v]) * weight(drow, jnp.int32(0) + k)
                high = full.astype(BF16)
                par[t * BLK : (t + 1) * BLK, :] += jnp.dot(high, eff[2, rows(mv), :], preferred_element_type=F32)
                far[rows(v), :] += gram(high, eff[1, rows(mt), :])
                return carry

            if t < nb - 1:
                lax.fori_loop(0, t + 1, z_pair, 0)
            else:
                for v in range(nb):
                    z_pair(jnp.int32(v), 0)
                    publish("far", v)

        lax.fori_loop(t, nb, x_pair, 0)
        publish("partner", t)
        publish("own", t)
        if t > 0:
            forward(0, t - 1)

    @pl.when(has_from)
    def _():
        for v in range(nb):
            relay("far", v)

    relay("partner", nb - 1)
    relay("own", nb - 1)

    loc_across.wait_recv()
    out_ref[...] = loc[:, my_cols] + lc_in[my_y] + ly_in[...]
    for t in range(nb - 1):
        out_ref[rows(mine(t)), :] += collect("own", t)

    @pl.when(has_from)
    def _():
        for v in range(nb):
            forward(1, v)

    forward(0, nb - 1)
    out_ref[rows(mine(nb - 1)), :] += collect("own", nb - 1)
    for t in range(nb):
        hop(0, t).wait_recv()
        out_ref[rows(other(t)), :] += hop_in[0, t].astype(F32)

    @pl.when(has_to)
    def _():
        for v in range(nb):
            hop(1, v).wait_recv()
            out_ref[rows(mine(v)), :] += hop_in[1, v].astype(F32)

    d_x.wait_send()
    e_x.wait_send()
    for t in range(nb - 2, nb):
        x_copies[t].wait_send()

    @pl.when(has_to)
    def _():
        d_z.wait_send()
        e_z.wait_send()
        for t in range(nb - 2, nb):
            z_copies[t].wait_send()

    for c in e_own + e_partner + [loc_core(0), loc_core(1), loc_across]:
        c.wait_send()
    for t in range(nb):
        for kind in ("own", "partner"):
            for c in to_core(kind, t) + [across(kind, t)]:
                c.wait_send()
        hop(0, t).wait_send()

    @pl.when(has_from)
    def _():
        for c in e_far:
            c.wait_send()
        for t in range(nb):
            for c in to_core("far", t) + [across("far", t)]:
                c.wait_send()
            hop(1, t).wait_send()


def body(n_genome, n_samp, dosage, effects, depth):
    nb = depth.shape[0]
    samples, variants = dosage.shape
    traits = effects.shape[1]
    all_traits = traits * n_samp
    half = samples // 2
    d = jnp.zeros((8, BLK), F32).at[:nb].set(jnp.broadcast_to(depth.astype(F32)[:, None], (nb, BLK)))
    dma = pltpu.SemaphoreType.DMA
    return pl.pallas_call(
        functools.partial(kernel, n_genome, n_samp, nb, half, traits, 1.0 / (samples * n_samp)),
        out_shape=jax.ShapeDtypeStruct((variants, traits), F32),
        in_specs=[
            pl.BlockSpec(memory_space=pl.ANY),
            pl.BlockSpec(memory_space=pl.ANY),
            pl.BlockSpec(memory_space=pltpu.VMEM),
        ],
        out_specs=pl.BlockSpec(memory_space=pltpu.VMEM),
        scratch_shapes=[
            pltpu.VMEM((nb, samples, BLK), BF16),
            pltpu.VMEM((nb, half, BLK), BF16),
            pltpu.VMEM((nb, half, BLK), BF16),
            pltpu.VMEM((3, variants, all_traits), BF16),
            pltpu.VMEM((2, 8, BLK), F32),
            pltpu.VMEM((variants, all_traits), F32),
            pltpu.VMEM((variants, all_traits), F32),
            pltpu.VMEM((variants, all_traits), F32),
            pltpu.VMEM((variants, all_traits), F32),
            pltpu.VMEM((2, variants, traits), F32),
            pltpu.VMEM((variants, traits), F32),
            pltpu.VMEM((variants, traits), F32),
            pltpu.VMEM((3, nb, 2, BLK, traits), F32),
            pltpu.VMEM((3, nb, BLK, traits), BF16),
            pltpu.VMEM((3, nb, BLK, traits), BF16),
            pltpu.VMEM((2, nb, BLK, traits), BF16),
            pltpu.VMEM((2, nb, BLK, traits), BF16),
            dma((nb,)), dma((1,)),
            dma((nb,)), dma((nb,)), dma((nb,)), dma((nb,)),
            dma((3, 3)), dma((3, 3)),
            dma((2,)), dma((2,)), dma((2,)), dma((2,)),
            dma((2,)), dma((2,)), dma((1,)), dma((1,)),
            dma((3, nb, 2)), dma((3, nb, 2)), dma((3, nb)), dma((3, nb)),
            dma((2, nb)), dma((2, nb)),
        ],
        compiler_params=pltpu.CompilerParams(
            collective_id=0, has_side_effects=True, vmem_limit_bytes=60 * 1024 * 1024
        ),
        cost_estimate=pl.CostEstimate(
            flops=2 * 20 * BLK * BLK * samples, bytes_accessed=4 * samples * variants, transcendentals=0
        ),
    )(dosage, effects, d)


def solution(mesh):
    return jax.shard_map(
        functools.partial(body, mesh.shape["genome"], mesh.shape["samp"]),
        mesh=mesh,
        in_specs=(P("samp", "genome"), P("genome", "samp"), P("genome")),
        out_specs=P("genome", "samp"),
        check_vma=False,
    )
```

```python
import functools

import jax
import jax.numpy as jnp
from jax import lax
from jax.experimental import pallas as pl
from jax.experimental.pallas import tpu as pltpu
from jax.sharding import PartitionSpec as P

BLK = 256
MESH = pl.DeviceIdType.MESH
F32 = jnp.float32
BF16 = jnp.bfloat16
CONTRACT0 = (((0,), (0,)), ((), ()))


def gram(left, right):
    return lax.dot_general(left, right, CONTRACT0, preferred_element_type=F32)


def kernel(
    n_genome, n_samp, nb, half, traits, scale,
    x_ref, e_ref, depth_ref, out_ref,
    d_ref, own, xbuf, zbuf, eff, dep, loc, cro, par, far, lc_in, ly_out, ly_in, c_in, y_out, y_in, hop_out, hop_in,
    own_sem, own_e_sem, x_send, x_recv, z_send, z_recv, es_send, es_recv, ex_send, ex_recv,
    ds_send, ds_recv, lc_send, lc_recv, ly_send, ly_recv, c_send, c_recv, y_send, y_recv, h_send, h_recv,
):
    g = lax.axis_index("genome")
    s = lax.axis_index("samp")
    q = lax.rem(g, 2)
    sign = 1 - 2 * q
    partner = g + sign
    z_from = g + 2 * sign
    z_to = g - 2 * sign
    has_from = jnp.logical_and(z_from >= 0, z_from < n_genome)
    has_to = jnp.logical_and(z_to >= 0, z_to < n_genome)

    def mine(u):
        return u + q * (nb - 1 - 2 * u)

    def other(u):
        return nb - 1 - mine(u)

    core = lax.rem(s, 2)
    core_mate = s + 1 - 2 * core
    cross_mate = lax.rem(s + 2, n_samp)

    def cols(t):
        return pl.ds(pl.multiple_of(t * traits, traits), traits)

    my_cols = cols(s)
    keep_rows = pl.ds(pl.multiple_of(q * half, half), half)
    give_rows = pl.ds(pl.multiple_of((1 - q) * half, half), half)

    def remote(src, dst, ss, rsem, gg, sss):
        return pltpu.make_async_remote_copy(
            src_ref=src, dst_ref=dst, send_sem=ss, recv_sem=rsem,
            device_id=(gg, sss), device_id_type=MESH,
        )

    barrier = pltpu.get_barrier_semaphore()
    for mate in (core_mate, cross_mate):
        pl.semaphore_signal(barrier, inc=1, device_id=(g, mate), device_id_type=MESH)
    pl.semaphore_signal(barrier, inc=1, device_id=(partner, s), device_id_type=MESH)

    @pl.when(has_from)
    def _():
        pl.semaphore_signal(barrier, inc=1, device_id=(z_from, s), device_id_type=MESH)

    @pl.when(has_to)
    def _():
        pl.semaphore_signal(barrier, inc=1, device_id=(z_to, s), device_id_type=MESH)

    own_copies = [
        pltpu.make_async_copy(x_ref.at[:, b * BLK : (b + 1) * BLK], own.at[b], own_sem.at[b])
        for b in range(nb)
    ]
    own_e = pltpu.make_async_copy(e_ref, eff.at[0, :, my_cols], own_e_sem.at[0])
    own_e.start()
    for c in own_copies:
        c.start()
    pl.semaphore_wait(
        barrier, 3 + has_from.astype(jnp.int32) + has_to.astype(jnp.int32)
    )

    for b in range(nb):
        d_ref[b : b + 1, :] = jnp.full((1, BLK), depth_ref[b].astype(F32))

    def block_cols(b):
        return pl.ds(pl.multiple_of(b * BLK, BLK), BLK)

    x_copies = [
        remote(x_ref.at[give_rows, block_cols(other(t))], xbuf.at[t], x_send.at[t], x_recv.at[t], partner, s)
        for t in range(nb)
    ]
    z_copies = [
        remote(x_ref.at[keep_rows, block_cols(mine(t))], zbuf.at[t], z_send.at[t], z_recv.at[t], z_to, s)
        for t in range(nb)
    ]
    d_x = remote(d_ref, dep.at[0], ds_send.at[0], ds_recv.at[0], partner, s)
    d_z = remote(d_ref, dep.at[1], ds_send.at[1], ds_recv.at[1], z_to, s)
    e_x = remote(e_ref, eff.at[1, :, my_cols], ex_send.at[0], ex_recv.at[0], partner, s)
    e_z = remote(e_ref, eff.at[2, :, my_cols], ex_send.at[1], ex_recv.at[1], z_to, s)
    d_x.start()
    e_x.start()
    x_copies[0].start()
    x_copies[1].start()

    @pl.when(has_to)
    def _():
        d_z.start()
        e_z.start()
        z_copies[0].start()
        z_copies[1].start()

    def gather(slot, source):
        across = cols(cross_mate)
        here = eff.at[slot, :, my_cols]
        there = eff.at[slot, :, across]
        return [
            remote(source, here, es_send.at[slot, 0], es_recv.at[slot, 0], g, core_mate),
            remote(source, here, es_send.at[slot, 1], es_recv.at[slot, 1], g, cross_mate),
            remote(there, there, es_send.at[slot, 2], es_recv.at[slot, 2], g, core_mate),
        ]

    e_own = gather(0, e_ref)
    e_partner = gather(1, eff.at[1, :, my_cols])
    e_far = gather(2, eff.at[2, :, my_cols])
    e_own[0].start()
    e_own[1].start()
    loc[...] = jnp.zeros_like(loc)
    cro[...] = jnp.zeros_like(cro)
    par[...] = jnp.zeros_like(par)
    far[...] = jnp.zeros_like(far)
    e_own[1].wait_recv()
    e_own[2].start()
    e_x.wait_recv()
    e_partner[0].start()
    e_partner[1].start()

    @pl.when(has_from)
    def _():
        e_z.wait_recv()
        e_far[0].start()
        e_far[1].start()

    own_e.wait()
    for c in own_copies:
        c.wait()
    e_own[0].wait_recv()
    e_own[2].wait_recv()

    def weight(drow, k):
        return jnp.where(drow >= k.astype(F32), F32(scale), F32(0.0))

    def rows(b):
        return pl.ds(pl.multiple_of(b * BLK, BLK), BLK)

    def local_row(i, carry):
        def local_pair(j, carry):
            full = gram(own[i, :half], own[j, :half]) + gram(own[i, half:], own[j, half:])
            full = full * weight(d_ref[pl.ds(i, 1), :], j - i)
            high = full.astype(BF16)
            low = (full - high.astype(F32)).astype(BF16)
            ej = eff[0, rows(j), :]
            loc[rows(i), :] += jnp.dot(high, ej, preferred_element_type=F32) + jnp.dot(
                low, ej, preferred_element_type=F32
            )

            @pl.when(j > i)
            def _():
                ei = eff[0, rows(i), :]
                loc[rows(j), :] += gram(high, ei) + gram(low, ei)

            return carry

        return lax.fori_loop(i, nb, local_pair, carry)

    lax.fori_loop(0, nb, local_row, 0)
    def loc_core(y):
        return remote(
            loc.at[:, cols(2 * y + 1 - core)], lc_in.at[y], lc_send.at[y], lc_recv.at[y], g, core_mate
        )

    loc_across = remote(ly_out, ly_in, ly_send.at[0], ly_recv.at[0], g, cross_mate)
    loc_core(0).start()
    loc_core(1).start()
    e_partner[1].wait_recv()
    e_partner[2].start()
    d_x.wait_recv()

    @pl.when(has_from)
    def _():
        e_far[1].wait_recv()
        e_far[2].start()
        d_z.wait_recv()

    my_y = s // 2
    mate_y = 1 - my_y
    loc_core(0).wait_recv()
    loc_core(1).wait_recv()
    ly_out[...] = loc[:, cols(cross_mate)] + lc_in[mate_y]
    loc_across.start()
    e_partner[0].wait_recv()
    e_partner[2].wait_recv()

    @pl.when(has_from)
    def _():
        e_far[0].wait_recv()
        e_far[2].wait_recv()

    kinds = {"own": (0, cro), "partner": (1, par), "far": (2, far)}

    def block_rows(t):
        return pl.ds(t * BLK, BLK)

    def to_core(kind, t):
        n, acc = kinds[kind]
        return [
            remote(
                acc.at[block_rows(t), cols(2 * y + 1 - core)], c_in.at[n, t, y],
                c_send.at[n, t, y], c_recv.at[n, t, y], g, core_mate,
            )
            for y in range(2)
        ]

    def across(kind, t):
        n, _ = kinds[kind]
        return remote(y_out.at[n, t], y_in.at[n, t], y_send.at[n, t], y_recv.at[n, t], g, cross_mate)

    def publish(kind, t):
        for c in to_core(kind, t):
            c.start()

    def relay(kind, t):
        n, acc = kinds[kind]
        for c in to_core(kind, t):
            c.wait_recv()
        y_out[n, t] = (acc[block_rows(t), cols(cross_mate)] + c_in[n, t, mate_y]).astype(BF16)
        across(kind, t).start()

    def collect(kind, t):
        n, acc = kinds[kind]
        across(kind, t).wait_recv()
        return acc[block_rows(t), my_cols] + c_in[n, t, my_y] + y_in[n, t].astype(F32)

    def hop(n, t):
        return remote(
            hop_out.at[n, t], hop_in.at[n, t], h_send.at[n, t], h_recv.at[n, t],
            partner if n == 0 else z_from, s,
        )

    def prepare(n, t):
        hop_out[n, t] = collect("partner" if n == 0 else "far", t).astype(BF16)

    def forward(n, t):
        prepare(n, t)
        hop(n, t).start()

    for t in range(nb):
        x_copies[t].wait_recv()
        if t == nb - 1:
            for j in range(nb - 2):
                hop(0, j).start()
        if t + 2 < nb:
            x_copies[t].wait_send()
            x_copies[t + 2].start()

            @pl.when(has_to)
            def _():
                z_copies[t].wait_send()
                z_copies[t + 2].start()

        def x_pair(u, carry):
            k = nb + t - u
            mu, mt = mine(u), mine(t)
            drow = jnp.where(q == 0, d_ref[pl.ds(mu, 1), :], dep[0, pl.ds(mt, 1), :])
            full = gram(own[mu, keep_rows, :], xbuf[t]) * weight(drow, k)
            high = full.astype(BF16)
            cro[rows(u), :] += jnp.dot(high, eff[1, rows(other(nb - 1 - t)), :], preferred_element_type=F32)
            par[t * BLK : (t + 1) * BLK, :] += gram(high, eff[0, rows(mu), :])
            return carry

        if t > 0:
            relay("partner", t - 1)
            relay("own", t - 1)

        @pl.when(has_from)
        def _():
            z_copies[t].wait_recv()

            def z_pair(v, carry):
                k = nb + v - t
                mt, mv = mine(t), mine(v)
                drow = jnp.where(q == 0, dep[0, pl.ds(mt, 1), :], dep[1, pl.ds(mv, 1), :])
                full = gram(xbuf[t], zbuf[v]) * weight(drow, jnp.int32(0) + k)
                high = full.astype(BF16)
                par[t * BLK : (t + 1) * BLK, :] += jnp.dot(high, eff[2, rows(mv), :], preferred_element_type=F32)
                far[rows(v), :] += gram(high, eff[1, rows(mt), :])
                return carry

            if t < nb - 1:
                lax.fori_loop(0, t + 1, z_pair, 0)
            else:
                for v in range(nb):
                    z_pair(jnp.int32(v), 0)
                    publish("far", v)

        lax.fori_loop(t, nb, x_pair, 0)
        publish("partner", t)
        publish("own", t)
        if 0 < t < nb - 1:
            prepare(0, t - 1)

    @pl.when(has_from)
    def _():
        for v in range(nb):
            relay("far", v)

    forward(0, nb - 2)
    relay("partner", nb - 1)
    relay("own", nb - 1)

    loc_across.wait_recv()
    out_ref[...] = loc[:, my_cols] + lc_in[my_y] + ly_in[...]
    for t in range(nb - 1):
        out_ref[rows(mine(t)), :] += collect("own", t)

    @pl.when(has_from)
    def _():
        for v in range(nb):
            forward(1, v)

    forward(0, nb - 1)
    out_ref[rows(mine(nb - 1)), :] += collect("own", nb - 1)
    for t in range(nb):
        hop(0, t).wait_recv()
        out_ref[rows(other(t)), :] += hop_in[0, t].astype(F32)

    @pl.when(has_to)
    def _():
        for v in range(nb):
            hop(1, v).wait_recv()
            out_ref[rows(mine(v)), :] += hop_in[1, v].astype(F32)

    d_x.wait_send()
    e_x.wait_send()
    for t in range(nb - 2, nb):
        x_copies[t].wait_send()

    @pl.when(has_to)
    def _():
        d_z.wait_send()
        e_z.wait_send()
        for t in range(nb - 2, nb):
            z_copies[t].wait_send()

    for c in e_own + e_partner + [loc_core(0), loc_core(1), loc_across]:
        c.wait_send()
    for t in range(nb):
        for kind in ("own", "partner"):
            for c in to_core(kind, t) + [across(kind, t)]:
                c.wait_send()
        hop(0, t).wait_send()

    @pl.when(has_from)
    def _():
        for c in e_far:
            c.wait_send()
        for t in range(nb):
            for c in to_core("far", t) + [across("far", t)]:
                c.wait_send()
            hop(1, t).wait_send()


def body(n_genome, n_samp, dosage, effects, depth):
    nb = depth.shape[0]
    samples, variants = dosage.shape
    traits = effects.shape[1]
    all_traits = traits * n_samp
    half = samples // 2
    dma = pltpu.SemaphoreType.DMA
    return pl.pallas_call(
        functools.partial(kernel, n_genome, n_samp, nb, half, traits, 1.0 / (samples * n_samp)),
        out_shape=jax.ShapeDtypeStruct((variants, traits), F32),
        in_specs=[
            pl.BlockSpec(memory_space=pl.ANY),
            pl.BlockSpec(memory_space=pl.ANY),
            pl.BlockSpec(memory_space=pltpu.SMEM),
        ],
        out_specs=pl.BlockSpec(memory_space=pltpu.VMEM),
        scratch_shapes=[
            pltpu.VMEM((8, BLK), F32),
            pltpu.VMEM((nb, samples, BLK), BF16),
            pltpu.VMEM((nb, half, BLK), BF16),
            pltpu.VMEM((nb, half, BLK), BF16),
            pltpu.VMEM((3, variants, all_traits), BF16),
            pltpu.VMEM((2, 8, BLK), F32),
            pltpu.VMEM((variants, all_traits), F32),
            pltpu.VMEM((variants, all_traits), F32),
            pltpu.VMEM((variants, all_traits), F32),
            pltpu.VMEM((variants, all_traits), F32),
            pltpu.VMEM((2, variants, traits), F32),
            pltpu.VMEM((variants, traits), F32),
            pltpu.VMEM((variants, traits), F32),
            pltpu.VMEM((3, nb, 2, BLK, traits), F32),
            pltpu.VMEM((3, nb, BLK, traits), BF16),
            pltpu.VMEM((3, nb, BLK, traits), BF16),
            pltpu.VMEM((2, nb, BLK, traits), BF16),
            pltpu.VMEM((2, nb, BLK, traits), BF16),
            dma((nb,)), dma((1,)),
            dma((nb,)), dma((nb,)), dma((nb,)), dma((nb,)),
            dma((3, 3)), dma((3, 3)),
            dma((2,)), dma((2,)), dma((2,)), dma((2,)),
            dma((2,)), dma((2,)), dma((1,)), dma((1,)),
            dma((3, nb, 2)), dma((3, nb, 2)), dma((3, nb)), dma((3, nb)),
            dma((2, nb)), dma((2, nb)),
        ],
        compiler_params=pltpu.CompilerParams(
            collective_id=0, has_side_effects=True, vmem_limit_bytes=60 * 1024 * 1024
        ),
        cost_estimate=pl.CostEstimate(
            flops=2 * 20 * BLK * BLK * samples, bytes_accessed=4 * samples * variants, transcendentals=0
        ),
    )(dosage, effects, depth)


def solution(mesh):
    return jax.shard_map(
        functools.partial(body, mesh.shape["genome"], mesh.shape["samp"]),
        mesh=mesh,
        in_specs=(P("samp", "genome"), P("genome", "samp"), P("genome")),
        out_specs=P("genome", "samp"),
        check_vma=False,
    )
```

```python
import functools

import jax
import jax.numpy as jnp
from jax import lax
from jax.experimental import pallas as pl
from jax.experimental.pallas import tpu as pltpu
from jax.sharding import PartitionSpec as P

BLK = 256
MESH = pl.DeviceIdType.MESH
F32 = jnp.float32
BF16 = jnp.bfloat16
CONTRACT0 = (((0,), (0,)), ((), ()))


def gram(left, right):
    return lax.dot_general(left, right, CONTRACT0, preferred_element_type=F32)


def kernel(
    n_genome, n_samp, nb, half, traits, scale,
    x_ref, e_ref, depth_ref, out_ref,
    d_ref, own, xbuf, zbuf, eff, dep, loc, cro, par, far, lc_in, ly_out, ly_in, c_in, y_out, y_in, hop_out, hop_in,
    own_sem, own_e_sem, x_send, x_recv, z_send, z_recv, es_send, es_recv, ex_send, ex_recv,
    ds_send, ds_recv, lc_send, lc_recv, ly_send, ly_recv, c_send, c_recv, y_send, y_recv, h_send, h_recv,
):
    g = lax.axis_index("genome")
    s = lax.axis_index("samp")
    q = lax.rem(g, 2)
    sign = 1 - 2 * q
    partner = g + sign
    z_from = g + 2 * sign
    z_to = g - 2 * sign
    has_from = jnp.logical_and(z_from >= 0, z_from < n_genome)
    has_to = jnp.logical_and(z_to >= 0, z_to < n_genome)

    def mine(u):
        return u + q * (nb - 1 - 2 * u)

    def other(u):
        return nb - 1 - mine(u)

    core = lax.rem(s, 2)
    core_mate = s + 1 - 2 * core
    cross_mate = lax.rem(s + 2, n_samp)

    def cols(t):
        return pl.ds(pl.multiple_of(t * traits, traits), traits)

    my_cols = cols(s)
    keep_rows = pl.ds(pl.multiple_of(q * half, half), half)
    give_rows = pl.ds(pl.multiple_of((1 - q) * half, half), half)

    def remote(src, dst, ss, rsem, gg, sss):
        return pltpu.make_async_remote_copy(
            src_ref=src, dst_ref=dst, send_sem=ss, recv_sem=rsem,
            device_id=(gg, sss), device_id_type=MESH,
        )

    barrier = pltpu.get_barrier_semaphore()
    for mate in (core_mate, cross_mate):
        pl.semaphore_signal(barrier, inc=1, device_id=(g, mate), device_id_type=MESH)
    pl.semaphore_signal(barrier, inc=1, device_id=(partner, s), device_id_type=MESH)

    @pl.when(has_from)
    def _():
        pl.semaphore_signal(barrier, inc=1, device_id=(z_from, s), device_id_type=MESH)

    @pl.when(has_to)
    def _():
        pl.semaphore_signal(barrier, inc=1, device_id=(z_to, s), device_id_type=MESH)

    own_copies = [
        pltpu.make_async_copy(x_ref.at[:, b * BLK : (b + 1) * BLK], own.at[b], own_sem.at[b])
        for b in range(nb)
    ]
    own_e = pltpu.make_async_copy(e_ref, eff.at[0, :, my_cols], own_e_sem.at[0])
    own_e.start()
    for c in own_copies:
        c.start()
    pl.semaphore_wait(
        barrier, 3 + has_from.astype(jnp.int32) + has_to.astype(jnp.int32)
    )

    for b in range(nb):
        d_ref[b : b + 1, :] = jnp.full((1, BLK), depth_ref[b].astype(F32))

    def block_cols(b):
        return pl.ds(pl.multiple_of(b * BLK, BLK), BLK)

    x_copies = [
        remote(x_ref.at[give_rows, block_cols(other(t))], xbuf.at[t], x_send.at[t], x_recv.at[t], partner, s)
        for t in range(nb)
    ]
    z_copies = [
        remote(x_ref.at[keep_rows, block_cols(mine(t))], zbuf.at[t], z_send.at[t], z_recv.at[t], z_to, s)
        for t in range(nb)
    ]
    d_x = remote(d_ref, dep.at[0], ds_send.at[0], ds_recv.at[0], partner, s)
    d_z = remote(d_ref, dep.at[1], ds_send.at[1], ds_recv.at[1], z_to, s)
    e_x = remote(e_ref, eff.at[1, :, my_cols], ex_send.at[0], ex_recv.at[0], partner, s)
    e_z = remote(e_ref, eff.at[2, :, my_cols], ex_send.at[1], ex_recv.at[1], z_to, s)
    d_x.start()
    e_x.start()
    x_copies[0].start()
    x_copies[1].start()

    @pl.when(has_to)
    def _():
        d_z.start()
        e_z.start()
        z_copies[0].start()
        z_copies[1].start()

    def gather(slot, source):
        across = cols(cross_mate)
        here = eff.at[slot, :, my_cols]
        there = eff.at[slot, :, across]
        return [
            remote(source, here, es_send.at[slot, 0], es_recv.at[slot, 0], g, core_mate),
            remote(source, here, es_send.at[slot, 1], es_recv.at[slot, 1], g, cross_mate),
            remote(there, there, es_send.at[slot, 2], es_recv.at[slot, 2], g, core_mate),
        ]

    e_own = gather(0, e_ref)
    e_partner = gather(1, eff.at[1, :, my_cols])
    e_far = gather(2, eff.at[2, :, my_cols])
    e_own[0].start()
    e_own[1].start()
    loc[...] = jnp.zeros_like(loc)
    cro[...] = jnp.zeros_like(cro)
    par[...] = jnp.zeros_like(par)
    far[...] = jnp.zeros_like(far)
    e_own[1].wait_recv()
    e_own[2].start()
    e_x.wait_recv()
    e_partner[0].start()
    e_partner[1].start()

    @pl.when(has_from)
    def _():
        e_z.wait_recv()
        e_far[0].start()
        e_far[1].start()

    own_e.wait()
    for c in own_copies:
        c.wait()
    e_own[0].wait_recv()
    e_own[2].wait_recv()

    def weight(drow, k):
        return jnp.where(drow >= k.astype(F32), F32(scale), F32(0.0))

    def rows(b):
        return pl.ds(pl.multiple_of(b * BLK, BLK), BLK)

    def local_row(i, carry):
        def local_pair(j, carry):
            full = gram(own[i, :half], own[j, :half]) + gram(own[i, half:], own[j, half:])
            full = full * weight(d_ref[pl.ds(i, 1), :], j - i)
            high = full.astype(BF16)
            low = (full - high.astype(F32)).astype(BF16)
            ej = eff[0, rows(j), :]
            loc[rows(i), :] += jnp.dot(high, ej, preferred_element_type=F32) + jnp.dot(
                low, ej, preferred_element_type=F32
            )

            @pl.when(j > i)
            def _():
                ei = eff[0, rows(i), :]
                loc[rows(j), :] += gram(high, ei) + gram(low, ei)

            return carry

        return lax.fori_loop(i, nb, local_pair, carry)

    lax.fori_loop(0, nb, local_row, 0)
    def loc_core(y):
        return remote(
            loc.at[:, cols(2 * y + 1 - core)], lc_in.at[y], lc_send.at[y], lc_recv.at[y], g, core_mate
        )

    loc_across = remote(ly_out, ly_in, ly_send.at[0], ly_recv.at[0], g, cross_mate)
    loc_core(0).start()
    loc_core(1).start()
    e_partner[1].wait_recv()
    e_partner[2].start()
    d_x.wait_recv()

    @pl.when(has_from)
    def _():
        e_far[1].wait_recv()
        e_far[2].start()
        d_z.wait_recv()

    my_y = s // 2
    mate_y = 1 - my_y
    loc_core(0).wait_recv()
    loc_core(1).wait_recv()
    ly_out[...] = loc[:, cols(cross_mate)] + lc_in[mate_y]
    loc_across.start()
    e_partner[0].wait_recv()
    e_partner[2].wait_recv()

    @pl.when(has_from)
    def _():
        e_far[0].wait_recv()
        e_far[2].wait_recv()

    kinds = {"own": (0, cro), "partner": (1, par), "far": (2, far)}

    def block_rows(t):
        return pl.ds(t * BLK, BLK)

    def to_core(kind, t):
        n, acc = kinds[kind]
        return [
            remote(
                acc.at[block_rows(t), cols(2 * y + 1 - core)], c_in.at[n, t, y],
                c_send.at[n, t, y], c_recv.at[n, t, y], g, core_mate,
            )
            for y in range(2)
        ]

    def across(kind, t):
        n, _ = kinds[kind]
        return remote(y_out.at[n, t], y_in.at[n, t], y_send.at[n, t], y_recv.at[n, t], g, cross_mate)

    def publish(kind, t):
        for c in to_core(kind, t):
            c.start()

    def relay(kind, t):
        n, acc = kinds[kind]
        for c in to_core(kind, t):
            c.wait_recv()
        y_out[n, t] = (acc[block_rows(t), cols(cross_mate)] + c_in[n, t, mate_y]).astype(BF16)
        across(kind, t).start()

    def collect(kind, t):
        n, acc = kinds[kind]
        across(kind, t).wait_recv()
        return acc[block_rows(t), my_cols] + c_in[n, t, my_y] + y_in[n, t].astype(F32)

    def hop(n, t):
        return remote(
            hop_out.at[n, t], hop_in.at[n, t], h_send.at[n, t], h_recv.at[n, t],
            partner if n == 0 else z_from, s,
        )

    def prepare(n, t):
        hop_out[n, t] = collect("partner" if n == 0 else "far", t).astype(BF16)

    def forward(n, t):
        prepare(n, t)
        hop(n, t).start()

    for t in range(nb):
        x_copies[t].wait_recv()
        if t == nb - 1:
            for j in range(nb - 2):
                hop(0, j).start()
        if t + 2 < nb:
            x_copies[t].wait_send()
            x_copies[t + 2].start()

            @pl.when(has_to)
            def _():
                z_copies[t].wait_send()
                z_copies[t + 2].start()

        def x_pair(u, carry):
            k = nb + t - u
            mu, mt = mine(u), mine(t)
            drow = jnp.where(q == 0, d_ref[pl.ds(mu, 1), :], dep[0, pl.ds(mt, 1), :])
            full = gram(own[mu, keep_rows, :], xbuf[t]) * weight(drow, k)
            high = full.astype(BF16)
            cro[rows(u), :] += jnp.dot(high, eff[1, rows(other(nb - 1 - t)), :], preferred_element_type=F32)
            par[t * BLK : (t + 1) * BLK, :] += gram(high, eff[0, rows(mu), :])
            return carry

        if t > 0:
            relay("partner", t - 1)
            relay("own", t - 1)

        if t == nb - 1:
            x_pair(jnp.int32(t), 0)
            publish("own", t)

        @pl.when(has_from)
        def _():
            if t < nb - 1:
                z_copies[t].wait_recv()

            def z_pair(v, carry):
                k = nb + v - t
                mt, mv = mine(t), mine(v)
                drow = jnp.where(q == 0, dep[0, pl.ds(mt, 1), :], dep[1, pl.ds(mv, 1), :])
                full = gram(xbuf[t], zbuf[v]) * weight(drow, jnp.int32(0) + k)
                high = full.astype(BF16)
                par[t * BLK : (t + 1) * BLK, :] += jnp.dot(high, eff[2, rows(mv), :], preferred_element_type=F32)
                far[rows(v), :] += gram(high, eff[1, rows(mt), :])
                return carry

            if t < nb - 1:
                lax.fori_loop(0, t + 1, z_pair, 0)
            else:
                for v in range(nb):
                    if v == t:
                        z_copies[t].wait_recv()
                    z_pair(jnp.int32(v), 0)
                    publish("far", v)
                    if v > 0:
                        relay("far", v - 1)

        if t < nb - 1:
            lax.fori_loop(t, nb, x_pair, 0)
        publish("partner", t)
        if t < nb - 1:
            publish("own", t)
        if 0 < t < nb - 1:
            prepare(0, t - 1)

    @pl.when(has_from)
    def _():
        relay("far", nb - 1)

    relay("partner", nb - 1)
    relay("own", nb - 1)
    forward(0, nb - 2)

    @pl.when(has_from)
    def _():
        for v in range(nb - 1):
            forward(1, v)

    loc_across.wait_recv()
    out_ref[...] = loc[:, my_cols] + lc_in[my_y] + ly_in[...]
    for t in range(nb - 1):
        out_ref[rows(mine(t)), :] += collect("own", t)

    @pl.when(has_from)
    def _():
        forward(1, nb - 1)

    forward(0, nb - 1)
    out_ref[rows(mine(nb - 1)), :] += collect("own", nb - 1)
    for t in range(nb):
        hop(0, t).wait_recv()
        out_ref[rows(other(t)), :] += hop_in[0, t].astype(F32)

    @pl.when(has_to)
    def _():
        for v in range(nb):
            hop(1, v).wait_recv()
            out_ref[rows(mine(v)), :] += hop_in[1, v].astype(F32)

    d_x.wait_send()
    e_x.wait_send()
    for t in range(nb - 2, nb):
        x_copies[t].wait_send()

    @pl.when(has_to)
    def _():
        d_z.wait_send()
        e_z.wait_send()
        for t in range(nb - 2, nb):
            z_copies[t].wait_send()

    for c in e_own + e_partner + [loc_core(0), loc_core(1), loc_across]:
        c.wait_send()
    for t in range(nb):
        for kind in ("own", "partner"):
            for c in to_core(kind, t) + [across(kind, t)]:
                c.wait_send()
        hop(0, t).wait_send()

    @pl.when(has_from)
    def _():
        for c in e_far:
            c.wait_send()
        for t in range(nb):
            for c in to_core("far", t) + [across("far", t)]:
                c.wait_send()
            hop(1, t).wait_send()


def body(n_genome, n_samp, dosage, effects, depth):
    nb = depth.shape[0]
    samples, variants = dosage.shape
    traits = effects.shape[1]
    all_traits = traits * n_samp
    half = samples // 2
    dma = pltpu.SemaphoreType.DMA
    return pl.pallas_call(
        functools.partial(kernel, n_genome, n_samp, nb, half, traits, 1.0 / (samples * n_samp)),
        out_shape=jax.ShapeDtypeStruct((variants, traits), F32),
        in_specs=[
            pl.BlockSpec(memory_space=pl.ANY),
            pl.BlockSpec(memory_space=pl.ANY),
            pl.BlockSpec(memory_space=pltpu.SMEM),
        ],
        out_specs=pl.BlockSpec(memory_space=pltpu.VMEM),
        scratch_shapes=[
            pltpu.VMEM((8, BLK), F32),
            pltpu.VMEM((nb, samples, BLK), BF16),
            pltpu.VMEM((nb, half, BLK), BF16),
            pltpu.VMEM((nb, half, BLK), BF16),
            pltpu.VMEM((3, variants, all_traits), BF16),
            pltpu.VMEM((2, 8, BLK), F32),
            pltpu.VMEM((variants, all_traits), F32),
            pltpu.VMEM((variants, all_traits), F32),
            pltpu.VMEM((variants, all_traits), F32),
            pltpu.VMEM((variants, all_traits), F32),
            pltpu.VMEM((2, variants, traits), F32),
            pltpu.VMEM((variants, traits), F32),
            pltpu.VMEM((variants, traits), F32),
            pltpu.VMEM((3, nb, 2, BLK, traits), F32),
            pltpu.VMEM((3, nb, BLK, traits), BF16),
            pltpu.VMEM((3, nb, BLK, traits), BF16),
            pltpu.VMEM((2, nb, BLK, traits), BF16),
            pltpu.VMEM((2, nb, BLK, traits), BF16),
            dma((nb,)), dma((1,)),
            dma((nb,)), dma((nb,)), dma((nb,)), dma((nb,)),
            dma((3, 3)), dma((3, 3)),
            dma((2,)), dma((2,)), dma((2,)), dma((2,)),
            dma((2,)), dma((2,)), dma((1,)), dma((1,)),
            dma((3, nb, 2)), dma((3, nb, 2)), dma((3, nb)), dma((3, nb)),
            dma((2, nb)), dma((2, nb)),
        ],
        compiler_params=pltpu.CompilerParams(
            collective_id=0, has_side_effects=True, vmem_limit_bytes=60 * 1024 * 1024
        ),
        cost_estimate=pl.CostEstimate(
            flops=2 * 20 * BLK * BLK * samples, bytes_accessed=4 * samples * variants, transcendentals=0
        ),
    )(dosage, effects, depth)


def solution(mesh):
    return jax.shard_map(
        functools.partial(body, mesh.shape["genome"], mesh.shape["samp"]),
        mesh=mesh,
        in_specs=(P("samp", "genome"), P("genome", "samp"), P("genome")),
        out_specs=P("genome", "samp"),
        check_vma=False,
    )
```
